32 devices in a mesh: row: 4 (over z), col: 8 (over y, x, core).
Axes of the slice: x: 2, y: 2, z: 4, core: 2. Of those that a mesh axis runs over, the one named last changes fastest.
Arguments:
- emb: bfloat16 [131072, 512], P(('row', 'col')), may hold values from -6 to 6
- tiles: bfloat16 [256, 4, 256, 256], P(('row', 'col')), may hold values from -0.375 to 0.375
- msg_src: int32 [256, 4], P(('row', 'col')), may hold values from 0 to 15
- msg_dst: int32 [256, 4], P(('row', 'col')), may hold values from 0 to 16, as said below
- msg_count: int32 [256, 4], P(('row', 'col')), may hold values from 1 to 256
- weight: bfloat16 [512, 512], replicated, may hold values from -0.25 to 0.25
- docs: bfloat16 [256, 512], P('row'), may hold values from -0.059814453 to 0.099609375
- doc_labels: int32 [256, 8], replicated, may hold values from 0 to 131071
Outputs:
- hidden: bfloat16 [131072, 512], P(('row', 'col'))
- grad_docs: float32 [256, 512], P('row')
- grad_weight: float32 [512, 512], replicated
The draws below stay inside these ranges and needn't reach their ends.
Inputs may be any that keep to these rules, and one draw needn't show every extreme that they name: For each sending device and each column of its row, the used slots (msg_dst below 16) come first and 16 marks an unused slot. In every row of devices some column receives all 4 slots used from every sender of that row.
All inputs are finite; a program needn't handle non-finite values.
Results may differ from the reference program's by a relative error of at most 0.0052.
Values may be sent and summed in bfloat16 or wider, within the bound.
A program may use at most 192 MiB of HBM per device.

```python
import jax
import jax.numpy as jnp
from jax import lax

D = 512
LABEL_DEV = 4096
BLK = 256
CAP = 4
POS = 8
BLK_DEV = 16
LABELS = 131072
DOCS = 256
N_ROW = 4
N_COL = 8


def draw_msg_dst(key, part):
    rows = N_ROW * N_COL * N_COL
    index = jnp.arange(rows, dtype=jnp.int32)
    sender = index // N_COL
    peer = index % N_COL
    row_of = sender // N_COL
    heavy = jax.random.randint(jax.random.fold_in(key, 11), (N_ROW * N_COL,), 0, 4) == 0
    light = jax.random.randint(jax.random.fold_in(key, 12), (rows,), 0, CAP // 2 + 1)
    full_col = jax.random.randint(jax.random.fold_in(key, 13), (N_ROW,), 0, N_COL)
    filled = jnp.where(heavy[sender] | (peer == full_col[row_of]), CAP, light)
    slot_ids = jnp.arange(CAP, dtype=jnp.int32)
    chosen = jax.random.randint(jax.random.fold_in(key, 14), (rows, CAP), 0, BLK_DEV)
    return jnp.where(slot_ids[None, :] < filled[:, None], chosen, BLK_DEV).astype(jnp.int32)


def with_ends(entries, rng, least, largest):
    place = [jax.random.randint(jax.random.fold_in(rng, axis), (), 0, length) for axis, length in enumerate(entries.shape)]
    widest = entries.shape.index(max(entries.shape))
    neighbour = place[:widest] + [(place[widest] + 1) % entries.shape[widest]] + place[widest + 1:]
    return entries.at[tuple(place)].set(least).at[tuple(neighbour)].set(largest)


def shard_levels(rng, shape, split, least, top_value):
    def one(dim, shards_of):
        heights = jax.random.uniform(jax.random.fold_in(jax.random.fold_in(rng, 6), dim), (shards_of,), jnp.float32, least / len(split), top_value / len(split))
        return jnp.repeat(jnp.exp(heights), shape[dim] // shards_of).reshape((-1,) + (1,) * (len(shape) - dim - 1))

    factor_of = one(*split[0])
    for cut in split[1:]:
        factor_of = factor_of * one(*cut)
    return factor_of


def centred(stream_key, extent, scale, most, split=(), kind=jnp.bfloat16):
    drawn = scale * jax.random.normal(stream_key, extent, jnp.float32)
    if split:
        drawn = drawn * shard_levels(stream_key, extent, split, -0.22, 0.18)
    return jnp.clip(drawn, -most, most).astype(kind)


def setup_inputs(seed: int = 0) -> dict:
    keys = jax.random.split(jax.random.key(seed), 9)
    return {
        "emb": centred(keys[0], (LABELS, D), 1.0, 6.0, ((0, 32),)),
        "tiles": centred(keys[1], (N_ROW * N_COL * N_COL, CAP, BLK, BLK), BLK ** -0.5, 0.375, ((0, 32),)),
        "msg_src": with_ends(jax.random.randint(keys[2], (N_ROW * N_COL * N_COL, CAP), 0, BLK_DEV), jax.random.fold_in(keys[2], 1), 0, BLK_DEV - 1).astype(jnp.int32),
        "msg_dst": draw_msg_dst(jax.random.fold_in(keys[8], 71), 0),
        "msg_count": with_ends(jax.random.randint(keys[4], (N_ROW * N_COL * N_COL, CAP), 1, BLK + 1), jax.random.fold_in(keys[4], 1), 1, BLK).astype(jnp.int32),
        "weight": centred(keys[5], (D, D), D ** -0.5, 0.25),
        "docs": jnp.clip(-0.059814453 + 0.15942383 * jax.random.uniform(keys[6], (DOCS, D), jnp.float32) ** shard_levels(keys[6], (DOCS, D), ((0, 4),), -0.2, 0.2), -0.059814453, 0.099609375).astype(jnp.bfloat16),
        "doc_labels": with_ends(jax.random.randint(keys[7], (DOCS, POS), 0, LABELS), jax.random.fold_in(keys[7], 1), 0, LABELS - 1).astype(jnp.int32),
    }


def reference(emb, tiles, msg_src, msg_dst, msg_count, weight, docs, doc_labels):
    n_dev = N_ROW * N_COL
    blocks = emb.reshape(n_dev, BLK_DEV, BLK, D)
    src_all = msg_src.reshape(n_dev, N_COL, CAP)
    dst_all = msg_dst.reshape(n_dev, N_COL, CAP)
    cnt_all = msg_count.reshape(n_dev, N_COL, CAP)
    tile_all = tiles.reshape(n_dev, N_COL, CAP, BLK, BLK)
    labels_total = float(LABEL_DEV * n_dev)
    block_ids = jnp.arange(BLK_DEV, dtype=jnp.int32)

    def one_device(carry, device):
        doc_sum, weight_sum = carry
        row_index = device // N_COL
        col_index = device % N_COL
        senders = row_index * N_COL + jnp.arange(N_COL, dtype=jnp.int32)
        source = src_all[senders, col_index]
        target = dst_all[senders, col_index]
        counts = cnt_all[senders, col_index].astype(jnp.float32)
        tile_set = tile_all[senders, col_index]
        picked = blocks[senders[:, None], source]
        messages = jnp.einsum("pqij,pqjd->pqid", tile_set.astype(jnp.float32),
                              picked.astype(jnp.float32)).astype(jnp.bfloat16)
        hot = (target[None, :, :] == block_ids[:, None, None]).astype(jnp.float32)
        weighted = hot * counts[None]
        total = jnp.einsum("bpq,pqid->bid", weighted, messages.astype(jnp.float32))
        total = total + float(BLK) * blocks[device].astype(jnp.float32)
        denom = float(BLK) + jnp.sum(weighted, axis=(1, 2))
        agg = (total / denom[:, None, None]).astype(jnp.bfloat16).reshape(LABEL_DEV, D)
        pre = jnp.dot(agg, weight, preferred_element_type=jnp.float32)
        hidden = jax.nn.silu(pre).astype(jnp.bfloat16)
        scores = jnp.dot(docs, hidden.T, preferred_element_type=jnp.float32)
        label_ids = device * LABEL_DEV + jnp.arange(LABEL_DEV, dtype=jnp.int32)
        positive = jnp.any(doc_labels[:, :, None] == label_ids[None, None, :], axis=1)
        prob = jax.nn.sigmoid(scores)
        dscore = jnp.where(positive, (prob - 1.0) / float(POS), prob / labels_total).astype(jnp.bfloat16)
        doc_part = jnp.dot(dscore, hidden, preferred_element_type=jnp.float32)
        dhid = jnp.dot(dscore.T, docs, preferred_element_type=jnp.float32)
        sig = jax.nn.sigmoid(pre)
        dpre = (dhid * sig * (1.0 + pre * (1.0 - sig))).astype(jnp.bfloat16)
        weight_part = jnp.dot(agg.T, dpre, preferred_element_type=jnp.float32)
        return (doc_sum + doc_part, weight_sum + weight_part), hidden

    start = (jnp.zeros((DOCS, D), jnp.float32), jnp.zeros((D, D), jnp.float32))
    (grad_docs, grad_weight), hiddens = lax.scan(one_device, start, jnp.arange(n_dev, dtype=jnp.int32))
    return hiddens.reshape(LABELS, D), grad_docs, grad_weight
```

```python
import jax
import jax.numpy as jnp
from jax import lax
from jax.sharding import PartitionSpec as P


def row_pieces(blk):
    unit = blk // 8
    return ((0, 3 * unit), (3 * unit, 6 * unit), (6 * unit, blk))


def per_device(emb, tiles, msg_src, msg_dst, msg_count, weight, docs, doc_labels):
    n_col = lax.axis_size("col")
    n_row = lax.axis_size("row")
    n_dev = n_row * n_col
    row = lax.axis_index("row")
    label_dev, width = emb.shape
    blk = tiles.shape[-1]
    cap = tiles.shape[1]
    blk_dev = label_dev // blk
    labels_total = float(label_dev * n_dev)
    pos_count = doc_labels.shape[1]
    own_blocks = emb.reshape(blk_dev, blk, width)
    device = row * n_col + lax.axis_index("col")

    meta = jnp.concatenate([msg_dst, msg_count], axis=1).astype(jnp.bfloat16)
    meta = lax.all_to_all(meta, "col", split_axis=0, concat_axis=0, tiled=True)
    picked = own_blocks[msg_src]

    pieces = row_pieces(blk)
    arrived = []
    for first, last in pieces:
        message = jnp.einsum(
            "pqij,pqjd->pqid", tiles[:, :, first:last], picked, preferred_element_type=jnp.float32
        ).astype(jnp.bfloat16)
        arrived.append(lax.all_to_all(message, "col", split_axis=0, concat_axis=0, tiled=True))

    all_docs = lax.all_gather(docs, "row", axis=0, tiled=True)
    slots_all = n_col * cap
    block_ids = jnp.arange(blk_dev, dtype=jnp.float32)
    meta = meta.astype(jnp.float32)
    dst_seen = meta[:, :cap].reshape(1, slots_all)
    cnt_seen = meta[:, cap:].reshape(1, slots_all)
    weighted = jnp.where(dst_seen == block_ids[:, None], cnt_seen, 0.0)
    denom = float(blk) + jnp.sum(weighted, axis=1)
    weighted = weighted.astype(jnp.bfloat16)

    hiddens = []
    doc_part = 0.0
    weight_part = 0.0
    for (first, last), received in zip(pieces, arrived):
        rows = last - first
        count = blk_dev * rows
        total = jnp.dot(
            weighted,
            received.reshape(slots_all, rows * width),
            preferred_element_type=jnp.float32,
        ).reshape(blk_dev, rows, width)
        total = total + float(blk) * own_blocks[:, first:last].astype(jnp.float32)
        agg = (total / denom[:, None, None]).astype(jnp.bfloat16).reshape(count, width)
        pre = jnp.dot(agg, weight, preferred_element_type=jnp.float32)
        hidden = jax.nn.silu(pre).astype(jnp.bfloat16)
        label_ids = (
            device * label_dev
            + blk * jnp.arange(blk_dev, dtype=jnp.int32)[:, None]
            + jnp.arange(first, last, dtype=jnp.int32)[None, :]
        ).reshape(count)
        scores = jnp.einsum("nd,ld->nl", all_docs, hidden, preferred_element_type=jnp.float32)
        positive = doc_labels[:, 0:1] == label_ids[None, :]
        for which in range(1, pos_count):
            positive = positive | (doc_labels[:, which : which + 1] == label_ids[None, :])
        prob = jax.nn.sigmoid(scores)
        dscore = jnp.where(
            positive, (prob - 1.0) / float(pos_count), prob / labels_total
        ).astype(jnp.bfloat16)
        doc_part = doc_part + jnp.dot(dscore, hidden, preferred_element_type=jnp.float32)
        dhid = jnp.einsum("nl,nd->ld", dscore, all_docs, preferred_element_type=jnp.float32)
        sig = jax.nn.sigmoid(pre)
        dpre = (dhid * sig * (1.0 + pre * (1.0 - sig))).astype(jnp.bfloat16)
        weight_part = weight_part + jnp.einsum(
            "la,lb->ab", agg, dpre, preferred_element_type=jnp.float32
        )
        hiddens.append(hidden.reshape(blk_dev, rows, width))
    hidden = jnp.concatenate(hiddens, axis=1).reshape(label_dev, width)

    doc_rows = doc_part.shape[0] // n_dev
    weight_rows = width // n_dev
    parts = jnp.concatenate(
        [
            weight_part.astype(jnp.bfloat16).reshape(n_dev, weight_rows, width),
            doc_part.astype(jnp.bfloat16).reshape(n_dev, doc_rows, width),
        ],
        axis=1,
    )
    parts = lax.all_to_all(parts, ("row", "col"), split_axis=0, concat_axis=0, tiled=True)
    share = jnp.sum(parts.astype(jnp.float32), axis=0).astype(jnp.bfloat16)
    shares = lax.all_to_all(
        jnp.broadcast_to(share[None], (n_dev,) + share.shape),
        ("row", "col"),
        split_axis=0,
        concat_axis=0,
        tiled=True,
    )
    grad_weight = shares[:, :weight_rows].reshape(width, width).astype(jnp.float32)
    own_row = lax.dynamic_slice_in_dim(shares, row * n_col, n_col, axis=0)
    grad_docs = own_row[:, weight_rows:].reshape(n_col * doc_rows, width).astype(jnp.float32)
    return (hidden, grad_docs, grad_weight)


def solution(mesh):
    in_specs = (
        P(("row", "col"), None),
        P(("row", "col"), None, None, None),
        P(("row", "col"), None),
        P(("row", "col"), None),
        P(("row", "col"), None),
        P(),
        P("row", None),
        P(),
    )
    out_specs = (P(("row", "col"), None), P("row", None), P())
    return jax.shard_map(
        per_device, mesh=mesh, in_specs=in_specs, out_specs=out_specs, check_vma=False
    )
```

```python
import jax
import jax.numpy as jnp
from jax import lax
from jax.sharding import PartitionSpec as P


def row_pieces(blk):
    unit = blk // 16
    return ((0, 8 * unit), (8 * unit, 13 * unit), (13 * unit, blk))


def per_device(emb, tiles, msg_src, msg_dst, msg_count, weight, docs, doc_labels):
    n_col = lax.axis_size("col")
    n_row = lax.axis_size("row")
    n_dev = n_row * n_col
    row = lax.axis_index("row")
    label_dev, width = emb.shape
    blk = tiles.shape[-1]
    cap = tiles.shape[1]
    blk_dev = label_dev // blk
    labels_total = float(label_dev * n_dev)
    pos_count = doc_labels.shape[1]
    own_blocks = emb.reshape(blk_dev, blk, width)
    col = lax.axis_index("col")
    device = row * n_col + col
    picked = own_blocks[msg_src]

    pieces = row_pieces(blk)
    meta = jnp.concatenate([msg_dst, msg_count], axis=1).astype(jnp.bfloat16)
    arrived = []
    for first, last in pieces:
        message = jnp.einsum(
            "pqij,pqjd->pqid", tiles[:, :, first:last], picked, preferred_element_type=jnp.float32
        ).astype(jnp.bfloat16)
        if arrived:
            message, arrived[-1] = lax.optimization_barrier((message, arrived[-1]))
        else:
            message, docs, meta = lax.optimization_barrier((message, docs, meta))
        arrived.append(lax.all_to_all(message, "col", split_axis=0, concat_axis=0, tiled=True))

    all_docs = lax.all_gather(docs, "row", axis=0, tiled=True)
    slots_all = n_col * cap
    block_ids = jnp.arange(blk_dev, dtype=jnp.float32)
    meta = lax.all_gather(meta, "col", axis=0)
    meta = lax.dynamic_index_in_dim(meta, col, axis=1, keepdims=False).astype(jnp.float32)
    dst_seen = meta[:, :cap].reshape(1, slots_all)
    cnt_seen = meta[:, cap:].reshape(1, slots_all)
    weighted = jnp.where(dst_seen == block_ids[:, None], cnt_seen, 0.0)
    denom = float(blk) + jnp.sum(weighted, axis=1)
    weighted = weighted.astype(jnp.bfloat16)

    hiddens = []
    doc_part = 0.0
    weight_part = 0.0
    for (first, last), received in zip(pieces, arrived):
        if hiddens:
            received, doc_part, weight_part = lax.optimization_barrier(
                (received, doc_part, weight_part)
            )
        rows = last - first
        count = blk_dev * rows
        total = jnp.dot(
            weighted,
            received.reshape(slots_all, rows * width),
            preferred_element_type=jnp.float32,
        ).reshape(blk_dev, rows, width)
        total = total + float(blk) * own_blocks[:, first:last].astype(jnp.float32)
        agg = (total / denom[:, None, None]).astype(jnp.bfloat16).reshape(count, width)
        pre = jnp.dot(agg, weight, preferred_element_type=jnp.float32)
        hidden = jax.nn.silu(pre).astype(jnp.bfloat16)
        label_ids = (
            device * label_dev
            + blk * jnp.arange(blk_dev, dtype=jnp.int32)[:, None]
            + jnp.arange(first, last, dtype=jnp.int32)[None, :]
        ).reshape(count)
        scores = jnp.einsum("nd,ld->nl", all_docs, hidden, preferred_element_type=jnp.float32)
        positive = doc_labels[:, 0:1] == label_ids[None, :]
        for which in range(1, pos_count):
            positive = positive | (doc_labels[:, which : which + 1] == label_ids[None, :])
        prob = jax.nn.sigmoid(scores)
        dscore = jnp.where(
            positive, (prob - 1.0) / float(pos_count), prob / labels_total
        ).astype(jnp.bfloat16)
        doc_part = doc_part + jnp.dot(dscore, hidden, preferred_element_type=jnp.float32)
        dhid = jnp.einsum("nl,nd->ld", dscore, all_docs, preferred_element_type=jnp.float32)
        sig = jax.nn.sigmoid(pre)
        dpre = (dhid * sig * (1.0 + pre * (1.0 - sig))).astype(jnp.bfloat16)
        weight_part = weight_part + jnp.einsum(
            "la,lb->ab", agg, dpre, preferred_element_type=jnp.float32
        )
        hiddens.append(hidden.reshape(blk_dev, rows, width))
    hidden = jnp.concatenate(hiddens, axis=1).reshape(label_dev, width)

    doc_rows = doc_part.shape[0] // n_dev
    weight_rows = width // n_dev
    parts = jnp.concatenate(
        [
            weight_part.astype(jnp.bfloat16).reshape(n_dev, weight_rows, width),
            doc_part.astype(jnp.bfloat16).reshape(n_dev, doc_rows, width),
        ],
        axis=1,
    )
    parts = lax.all_to_all(parts, ("row", "col"), split_axis=0, concat_axis=0, tiled=True)
    share = jnp.sum(parts.astype(jnp.float32), axis=0).astype(jnp.bfloat16)
    shares = lax.all_to_all(
        jnp.broadcast_to(share[None], (n_dev,) + share.shape),
        ("row", "col"),
        split_axis=0,
        concat_axis=0,
        tiled=True,
    )
    grad_weight = shares[:, :weight_rows].reshape(width, width).astype(jnp.float32)
    own_row = lax.dynamic_slice_in_dim(shares, row * n_col, n_col, axis=0)
    grad_docs = own_row[:, weight_rows:].reshape(n_col * doc_rows, width).astype(jnp.float32)
    return (hidden, grad_docs, grad_weight)


def solution(mesh):
    in_specs = (
        P(("row", "col"), None),
        P(("row", "col"), None, None, None),
        P(("row", "col"), None),
        P(("row", "col"), None),
        P(("row", "col"), None),
        P(),
        P("row", None),
        P(),
    )
    out_specs = (P(("row", "col"), None), P("row", None), P())
    return jax.shard_map(
        per_device, mesh=mesh, in_specs=in_specs, out_specs=out_specs, check_vma=False
    )
```

```python
import jax
import jax.numpy as jnp
from jax import lax
from jax.sharding import PartitionSpec as P


def row_pieces(blk):
    unit = blk // 16
    return ((0, 7 * unit), (7 * unit, 13 * unit), (13 * unit, blk))


def per_device(emb, tiles, msg_src, msg_dst, msg_count, weight, docs, doc_labels):
    n_col = lax.axis_size("col")
    n_row = lax.axis_size("row")
    n_dev = n_row * n_col
    row = lax.axis_index("row")
    label_dev, width = emb.shape
    blk = tiles.shape[-1]
    cap = tiles.shape[1]
    blk_dev = label_dev // blk
    labels_total = float(label_dev * n_dev)
    pos_count = doc_labels.shape[1]
    own_blocks = emb.reshape(blk_dev, blk, width)
    device = row * n_col + lax.axis_index("col")
    picked = own_blocks[msg_src]

    pieces = row_pieces(blk)
    meta = jnp.concatenate([msg_dst, msg_count], axis=1).astype(jnp.bfloat16)
    meta = lax.all_to_all(meta, "col", split_axis=0, concat_axis=0, tiled=True)
    arrived = []
    for first, last in pieces:
        message = jnp.einsum(
            "pqij,pqjd->pqid", tiles[:, :, first:last], picked, preferred_element_type=jnp.float32
        ).astype(jnp.bfloat16)
        if arrived:
            message, arrived[-1] = lax.optimization_barrier((message, arrived[-1]))
        else:
            message, docs, meta = lax.optimization_barrier((message, docs, meta))
        arrived.append(lax.all_to_all(message, "col", split_axis=0, concat_axis=0, tiled=True))

    all_docs = lax.all_gather(docs, "row", axis=0, tiled=True)
    slots_all = n_col * cap
    block_ids = jnp.arange(blk_dev, dtype=jnp.float32)
    meta = meta.astype(jnp.float32)
    dst_seen = meta[:, :cap].reshape(1, slots_all)
    cnt_seen = meta[:, cap:].reshape(1, slots_all)
    weighted = jnp.where(dst_seen == block_ids[:, None], cnt_seen, 0.0)
    denom = float(blk) + jnp.sum(weighted, axis=1)
    weighted = weighted.astype(jnp.bfloat16)

    hiddens = []
    doc_part = 0.0
    weight_part = 0.0
    for (first, last), received in zip(pieces, arrived):
        if hiddens:
            received, doc_part, weight_part = lax.optimization_barrier(
                (received, doc_part, weight_part)
            )
        rows = last - first
        count = blk_dev * rows
        total = jnp.dot(
            weighted,
            received.reshape(slots_all, rows * width),
            preferred_element_type=jnp.float32,
        ).reshape(blk_dev, rows, width)
        total = total + float(blk) * own_blocks[:, first:last].astype(jnp.float32)
        agg = (total / denom[:, None, None]).astype(jnp.bfloat16).reshape(count, width)
        pre = jnp.dot(agg, weight, preferred_element_type=jnp.float32)
        hidden = jax.nn.silu(pre).astype(jnp.bfloat16)
        label_ids = (
            device * label_dev
            + blk * jnp.arange(blk_dev, dtype=jnp.int32)[:, None]
            + jnp.arange(first, last, dtype=jnp.int32)[None, :]
        ).reshape(count)
        scores = jnp.einsum("nd,ld->nl", all_docs, hidden, preferred_element_type=jnp.float32)
        positive = doc_labels[:, 0:1] == label_ids[None, :]
        for which in range(1, pos_count):
            positive = positive | (doc_labels[:, which : which + 1] == label_ids[None, :])
        prob = jax.nn.sigmoid(scores)
        dscore = jnp.where(
            positive, (prob - 1.0) / float(pos_count), prob / labels_total
        ).astype(jnp.bfloat16)
        doc_part = doc_part + jnp.dot(dscore, hidden, preferred_element_type=jnp.float32)
        dhid = jnp.einsum("nl,nd->ld", dscore, all_docs, preferred_element_type=jnp.float32)
        sig = jax.nn.sigmoid(pre)
        dpre = (dhid * sig * (1.0 + pre * (1.0 - sig))).astype(jnp.bfloat16)
        weight_part = weight_part + jnp.einsum(
            "la,lb->ab", agg, dpre, preferred_element_type=jnp.float32
        )
        hiddens.append(hidden.reshape(blk_dev, rows, width))
    hidden = jnp.concatenate(hiddens, axis=1).reshape(label_dev, width)

    doc_rows = doc_part.shape[0] // n_dev
    weight_rows = width // n_dev
    parts = jnp.concatenate(
        [
            weight_part.astype(jnp.bfloat16).reshape(n_dev, weight_rows, width),
            doc_part.astype(jnp.bfloat16).reshape(n_dev, doc_rows, width),
        ],
        axis=1,
    )
    parts = lax.all_to_all(parts, ("row", "col"), split_axis=0, concat_axis=0, tiled=True)
    share = jnp.sum(parts.astype(jnp.float32), axis=0).astype(jnp.bfloat16)
    shares = lax.all_to_all(
        jnp.broadcast_to(share[None], (n_dev,) + share.shape),
        ("row", "col"),
        split_axis=0,
        concat_axis=0,
        tiled=True,
    )
    grad_weight = shares[:, :weight_rows].reshape(width, width).astype(jnp.float32)
    own_row = lax.dynamic_slice_in_dim(shares, row * n_col, n_col, axis=0)
    grad_docs = own_row[:, weight_rows:].reshape(n_col * doc_rows, width).astype(jnp.float32)
    return (hidden, grad_docs, grad_weight)


def solution(mesh):
    in_specs = (
        P(("row", "col"), None),
        P(("row", "col"), None, None, None),
        P(("row", "col"), None),
        P(("row", "col"), None),
        P(("row", "col"), None),
        P(),
        P("row", None),
        P(),
    )
    out_specs = (P(("row", "col"), None), P("row", None), P())
    return jax.shard_map(
        per_device, mesh=mesh, in_specs=in_specs, out_specs=out_specs, check_vma=False
    )
```
